256 devices in a mesh: dp: 4 (over x), seq: 64 (over y, z, core).
Axes of the slice: x: 4, y: 4, z: 8, core: 2. Of those that a mesh axis runs over, the one named last changes fastest.
Arguments:
- bases: int32 [4, 24576], P('dp', 'seq'), may hold values from 0 to 3
- gene_of_stretch: int32 [4, 64], P('dp', 'seq'), may hold values from 0 to 7, never falling along the last dimension, each value on 1 to 32 neighbouring positions
- embed_table: float32 [4, 512], replicated, may hold values from -6 to 6
- kernel_first_block: bfloat16 [11, 512, 512], replicated, may hold values from -0.078125 to 0.078125
- kernel_second_block: bfloat16 [11, 512, 512], replicated, may hold values from -0.078125 to 0.078125
- cotangent: bfloat16 [4, 24576, 512], P('dp', 'seq'), may hold values from -6 to 6
Outputs:
- features: bfloat16 [4, 24576, 512], P('dp', 'seq')
- first_kernel_gradient: float32 [11, 512, 512], P(None, 'seq', 'dp')
- second_kernel_gradient: float32 [11, 512, 512], P(None, 'seq', 'dp')
The draws below stay inside these ranges and needn't reach their ends.
Inputs may be any that keep to these rules, and one draw needn't show every extreme that they name: `gene_of_stretch`: along each group the gene numbers never fall; each gene covers consecutive stretches, and one gene covers 64 // 2 stretches.
All inputs are finite; a program needn't handle non-finite values.
Results may differ from the reference program's by a relative error of at most 0.0023.
The reference program's roundings to bfloat16 on the way count: a program that leaves them out, or rounds other values in their place, can miss the bound.
Values may be sent and summed in bfloat16 or wider, within the bound.
A program may use at most 128 MiB of HBM per device.

```python
import math
import jax
import jax.numpy as jnp
import numpy as np
from jax import lax

C = 512
KTAP = 11
DILATION_FIRST = 4
DILATION_SECOND = 25
STRETCH = 384
GROUPS = 4
STRETCHES = 64
LENGTH = 24576


def touch_ends(entries, rng, smallest, largest):
    index_at = [jax.random.randint(jax.random.fold_in(rng, axis), (), 0, length) for axis, length in enumerate(entries.shape)]
    widest = entries.shape.index(max(entries.shape))
    neighbour = index_at[:widest] + [(index_at[widest] + 1) % entries.shape[widest]] + index_at[widest + 1:]
    return entries.at[tuple(index_at)].set(smallest).at[tuple(neighbour)].set(largest)


def level_of(stream_key, dims, pieces, smallest, largest):
    level = 1.0
    for position, shards_of in pieces:
        heights = jax.random.uniform(jax.random.fold_in(jax.random.fold_in(stream_key, 6), position), (shards_of,), jnp.float32, smallest / len(pieces), largest / len(pieces))
        level = level * jnp.repeat(jnp.exp(heights), dims[position] // shards_of).reshape((-1,) + (1,) * (len(dims) - 1 - position))
    return level


def split_up(number_of, total, reach, slope):
    weights = [(1 << 20) // math.isqrt(standing ** slope) + 1 for standing in range(2, number_of + 1)]
    spare, holding = total - reach - (number_of - 1), [1] * (number_of - 1)
    while spare > 0:
        free = [i for i in range(number_of - 1) if holding[i] < reach]
        pool, remaining = sum([weights[i] for i in free]), spare
        for i in free:
            more = min(reach - holding[i], max(1, remaining * weights[i] // pool), spare)
            holding[i] = holding[i] + more
            spare = spare - more
    return np.array([reach] + holding)


def uneven(key, number_of, total, bound, skew):
    if number_of == 2:
        one = jax.random.randint(key, (), max(1, total - bound), min(bound, total - 1) + 1)
        return jnp.stack([one, total - one])
    tallies = jnp.asarray(split_up(number_of, total, bound, skew), jnp.int32)
    twos = (number_of - 1) // 2
    source_of, receiver = tallies[1:1 + 2 * twos:2], tallies[2:2 + 2 * twos:2]
    slack = jnp.minimum(source_of - 1, bound - receiver)
    moved = jax.random.randint(jax.random.fold_in(key, 1), (twos,), 0, 1 << 20) % (slack + 1)
    tallies = tallies.at[1:1 + 2 * twos:2].set(source_of - moved).at[2:2 + 2 * twos:2].set(receiver + moved)
    return tallies[jax.random.permutation(jax.random.fold_in(key, 2), number_of)]


def noise(key, dims, spread, reach, shards=(), held_as=jnp.bfloat16):
    gain = level_of(key, dims, shards, -0.22, 0.18) if shards else 1.0
    array = jax.random.normal(key, dims, jnp.float32) * spread * gain
    return jnp.minimum(jnp.maximum(array, -reach), reach).astype(held_as)


def setup_inputs(seed: int = 0) -> dict:
    streams_of = jax.random.split(jax.random.key(seed), 7)
    return {
        "bases": touch_ends(jax.random.randint(streams_of[0], (GROUPS, LENGTH), 0, 4), jax.random.fold_in(streams_of[0], 1), 0, 3).astype(jnp.int32),
        "gene_of_stretch": jax.vmap(lambda own: jnp.searchsorted(jnp.cumsum(uneven(own, max(2, STRETCHES // 8), STRETCHES, STRETCHES // 2, 2)), jnp.arange(STRETCHES), side="right"))(jax.random.split(streams_of[1], GROUPS)).reshape((GROUPS, STRETCHES)).astype(jnp.int32),
        "embed_table": noise(streams_of[2], (4, C), 1.0, 6.0, (), jnp.float32),
        "kernel_first_block": noise(streams_of[3], (KTAP, C, C), (KTAP * C) ** -0.5, 0.078125),
        "kernel_second_block": noise(streams_of[4], (KTAP, C, C), (KTAP * C) ** -0.5, 0.078125),
        "cotangent": noise(streams_of[5], (GROUPS, LENGTH, C), 1.0, 6.0, ((0, 4), (1, 64))),
    }


def shifted(values, label_rows, offset, pad):
    row_values = label_rows.shape[1]
    padded = jnp.pad(values, ((0, 0), (pad, pad), (0, 0)))
    padded_labels = jnp.pad(label_rows, ((0, 0), (pad, pad)))
    source = padded[:, pad + offset:pad + offset + row_values]
    keep = padded_labels[:, pad + offset:pad + offset + row_values] == label_rows
    return jnp.where(keep[:, :, None], source, jnp.zeros_like(source))


def convolve_forward(values, label_rows, kernel, dilation):
    pad = 5 * abs(dilation)
    total = jnp.zeros(values.shape, jnp.float32)
    for k in range(KTAP):
        stretch_part = shifted(values, label_rows, (k - KTAP // 2) * dilation, pad)
        flat = jnp.dot(stretch_part.reshape(-1, values.shape[2]), kernel[k], preferred_element_type=jnp.float32)
        total = total + flat.reshape(values.shape)
    return total


def convolve_backward(gradient_list, label_rows, kernel, dilation):
    pad = 5 * dilation
    total = jnp.zeros(gradient_list.shape, jnp.float32)
    for k in range(KTAP):
        stretch_part = shifted(gradient_list, label_rows, -(k - KTAP // 2) * dilation, pad)
        flat = jnp.dot(stretch_part.reshape(-1, gradient_list.shape[2]), kernel[k].T, preferred_element_type=jnp.float32)
        total = total + flat.reshape(gradient_list.shape)
    return total


def kernel_gradient(values, label_rows, gradient_list, dilation):
    pad = 5 * dilation
    block_output = []
    for k in range(KTAP):
        stretch_part = shifted(values, label_rows, (k - KTAP // 2) * dilation, pad)
        block_output.append(jnp.einsum("beh,beo->ho", stretch_part.astype(jnp.float32), gradient_list.astype(jnp.float32), precision=lax.Precision.HIGHEST))
    return jnp.stack(block_output)


def reference(bases, gene_of_stretch, embed_table, kernel_first_block, kernel_second_block, cotangent):
    label_rows = jnp.repeat(gene_of_stretch + 1, STRETCH, axis=1).astype(jnp.int32)
    hidden_input = jnp.take(embed_table, bases, axis=0).astype(jnp.bfloat16)
    activation_first = jnp.maximum(hidden_input, 0)
    hidden_first = (hidden_input.astype(jnp.float32) + convolve_forward(activation_first, label_rows, kernel_first_block, DILATION_FIRST)).astype(jnp.bfloat16)
    activation_second = jnp.maximum(hidden_first, 0)
    features = (hidden_first.astype(jnp.float32) + convolve_forward(activation_second, label_rows, kernel_second_block, DILATION_SECOND)).astype(jnp.bfloat16)
    second_kernel_gradient = kernel_gradient(activation_second, label_rows, cotangent, DILATION_SECOND)
    backward_second = convolve_backward(cotangent, label_rows, kernel_second_block, DILATION_SECOND)
    delta_first = (cotangent.astype(jnp.float32) + jnp.where(hidden_first > 0, backward_second, 0.0)).astype(jnp.bfloat16)
    first_kernel_gradient = kernel_gradient(activation_first, label_rows, delta_first, DILATION_FIRST)
    return features, first_kernel_gradient, second_kernel_gradient
```

```python
import jax
import jax.numpy as jnp
from jax import lax
from jax.experimental import pallas as pl
from jax.experimental.pallas import tpu as pltpu
from jax.sharding import PartitionSpec as P

MESH = pl.DeviceIdType.MESH
KTAP = 11
DILATION_FIRST = 4
DILATION_SECOND = 25
NX, NY, NZ, NC = 4, 4, 8, 2
SEQ = NY * NZ * NC
CH = 512
ROWS = 384
PAD = 128
EXT = ROWS + 2 * PAD
SLICE = CH // (NX * NY)
WIDE = 384
GROUP = NX * NY
HALF = CH // NC
ZROWS = HALF // NZ
F32, BF16 = jnp.float32, jnp.bfloat16


def kernel(
    bases, gene, table, cot, w1_hbm, w2_hbm,
    feat, out1, out2,
    w1, w2, gvm, gf, gt, gbuf, vown, vbuf, tsc, t3, t3t, a1t, ohs, x1b, a2f, acc, fvm,
    st, sbuf, a2s, gs, part, crecv, screcv, zrecv, szrecv, zs, ssum, yrecv, syrecv,
    wsem, w2sem, lsem, hs, hr, vs, vr, gss, gsr, bs, br, ssend, srecv, cs, cr, zsend, zrsem, ys, yr,
):
    x = lax.axis_index("dp")
    seq = lax.axis_index("seq")
    core = seq % NC
    z = (seq // NC) % NZ
    y = seq // (NC * NZ)
    left, right = (seq + SEQ - 1) % SEQ, (seq + 1) % SEQ

    def at(px, py, pz, pc):
        return {"dp": px, "seq": (py * NZ + pz) * NC + pc}

    def remote(src, dst, ssem, rsem, device):
        return pltpu.make_async_remote_copy(
            src_ref=src, dst_ref=dst, send_sem=ssem, recv_sem=rsem, device_id=device, device_id_type=MESH
        )

    load_g = pltpu.make_async_copy(cot.at[0], gvm.at[pl.ds(PAD, ROWS)], lsem.at[0])
    load_g.start()
    load_w1 = [pltpu.make_async_copy(w1_hbm.at[k], w1.at[k], wsem.at[k]) for k in range(KTAP)]
    load_w2 = [pltpu.make_async_copy(w2_hbm.at[k], w2.at[k], w2sem.at[k]) for k in range(KTAP)]
    for copy in load_w1 + load_w2:
        copy.start()

    group = [((x + d // NY) % NX, (y + d % NY) % NY) for d in range(GROUP)]
    partners = [{"dp": x, "seq": left}, {"dp": x, "seq": right}, at(x, y, z, 1 - core)]
    partners += [at(px, py, z, core) for px, py in group[1:]]
    partners += [at(x, y, (z + d) % NZ, core) for d in range(1, NZ)]
    barrier = pltpu.get_barrier_semaphore()
    for device in partners:
        pl.semaphore_signal(barrier, inc=1, device_id=device, device_id_type=MESH)

    label4 = 4.0 * gene[...].astype(F32)
    vown[1] = jnp.broadcast_to(bases[...].astype(F32) + label4, (8, ROWS))
    load_g.wait()
    own_g = gvm[PAD:PAD + ROWS, :]
    gt[...] = own_g.astype(F32).T.astype(BF16)
    pl.semaphore_wait(barrier, len(partners))

    v_copies = [
        remote(vown.at[1], vown.at[0], vs.at[0], vr.at[0], {"dp": x, "seq": right}),
        remote(vown.at[1], vown.at[2], vs.at[1], vr.at[1], {"dp": x, "seq": left}),
    ]
    h_copies = [
        remote(gvm.at[pl.ds(ROWS, PAD)], gvm.at[pl.ds(0, PAD)], hs.at[0], hr.at[0], {"dp": x, "seq": right}),
        remote(gvm.at[pl.ds(PAD, PAD)], gvm.at[pl.ds(PAD + ROWS, PAD)], hs.at[1], hr.at[1], {"dp": x, "seq": left}),
    ]

    def channels_of(px, py):
        return pl.ds(pl.multiple_of(px * (NY * SLICE) + py * SLICE, SLICE), SLICE)

    g_copies = [
        remote(gt.at[channels_of(*group[d])], gbuf.at[d], gss.at[d], gsr.at[d], at(*group[d], z, core))
        for d in range(1, GROUP)
    ]
    for copy in v_copies + h_copies + g_copies:
        copy.start()
    gbuf[0] = gt[channels_of(x, y), :]

    tab = table[...].astype(BF16).astype(F32)
    act = jnp.concatenate([jnp.maximum(tab, 0.0), jnp.zeros((12, CH), F32)], axis=0)
    a1t[...] = act.T
    act = act.astype(BF16)
    tsc[...] = jnp.zeros_like(tsc)
    for k in range(KTAP):
        load_w1[k].wait()
        seen = jnp.dot(act, w1[k], preferred_element_type=F32)
        for b in range(4):
            row = seen[b:b + 1, :]
            if k == KTAP // 2:
                row = row + tab[b:b + 1, :]
            at_row = b * 16 + KTAP - 1 - k
            tsc[at_row:at_row + 1, :] = row
    whole = tsc[...]
    high = whole.astype(BF16).astype(F32)
    middle = (whole - high).astype(BF16).astype(F32)
    low = whole - high - middle
    thirds = jnp.concatenate([high, middle, low], axis=0)
    t3[...] = thirds.astype(BF16)
    turned = thirds.T
    order = [(yy * NZ + zz) * NC + cc for cc in range(NC) for zz in range(NZ) for yy in range(NY)]
    t3t[...] = jnp.concatenate([turned[8 * s:8 * s + 8, :] for s in order], axis=0).astype(BF16)

    for copy in v_copies:
        copy.wait_recv()
    v_left = jnp.where(seq == 0, -64.0, vown[0])
    v_right = jnp.where(seq == SEQ - 1, -64.0, vown[2])
    v_all = jnp.concatenate([v_left, vown[1], v_right], axis=1)
    ahead = PAD + 5 * DILATION_FIRST
    v_all = v_all[0:1, ahead:ahead + 7 * PAD]
    tiles = [v_all[:, PAD * r:PAD * (r + 1)] for r in range(7)]
    vbuf[0] = jnp.concatenate(tiles + [jnp.broadcast_to(label4, (1, PAD))], axis=0)
    b_copies = [
        remote(vbuf.at[0], vbuf.at[d], bs.at[d], br.at[d], at(*group[d], z, core)) for d in range(1, GROUP)
    ]
    for copy in b_copies:
        copy.start()

    def onehot(block):
        lanes = jnp.concatenate([block[r:r + 1, :] for r in range(7)], axis=1)
        own = block[7:8, 0:1]
        shifted = pltpu.roll(jnp.broadcast_to(lanes, (16, 7 * PAD)), 0, 1, stride=DILATION_FIRST, stride_axis=0)
        shifted = shifted[:, PAD:PAD + EXT]
        relative = shifted[5:6, :] - own
        own = jnp.where((relative >= 0.0) & (relative < 4.0), own, 1000.0)
        relative = shifted - own
        return jnp.concatenate([jnp.where(relative == float(b), 1.0, 0.0) for b in range(4)], axis=0)

    own_hot = onehot(vbuf[0])
    hot_rows = own_hot.T
    hot_rows = jnp.concatenate([hot_rows, hot_rows, hot_rows], axis=1).astype(BF16)
    x1 = jnp.dot(hot_rows, t3[...], preferred_element_type=F32).astype(BF16)
    x1b[...] = x1[PAD:PAD + ROWS, :]
    a2f[...] = jnp.maximum(x1.astype(F32), 0.0)

    for copy in h_copies:
        copy.wait_recv()
    keep_left = jnp.where(jnp.floor(v_left[0:1, 0:1] * 0.25) * 4.0 == label4, 1.0, 0.0)
    keep_right = jnp.where(jnp.floor(v_right[0:1, 0:1] * 0.25) * 4.0 == label4, 1.0, 0.0)
    gf[0:PAD, :] = gvm[0:PAD, :].astype(F32) * keep_left
    gf[PAD:PAD + ROWS, :] = own_g.astype(F32)
    gf[PAD + ROWS:, :] = gvm[PAD + ROWS:, :].astype(F32) * keep_right
    for copy in load_w2:
        copy.wait()
    for k in range(KTAP):
        start = PAD - (k - KTAP // 2) * DILATION_SECOND
        term = lax.dot_general(
            gf[start:start + ROWS, :].astype(BF16), w2[k], (((1,), (1,)), ((), ())), preferred_element_type=F32
        )
        acc[...] = term if k == 0 else acc[...] + term
    dx1 = (gf[PAD:PAD + ROWS, :] + jnp.where(x1b[...].astype(F32) > 0.0, acc[...], 0.0)).astype(BF16)
    sums = jnp.dot(own_hot[:, PAD:PAD + ROWS].astype(BF16), dx1, preferred_element_type=F32)
    st[...] = jnp.concatenate([sums, jnp.zeros_like(sums)], axis=0).T
    s_copies = [
        remote(st.at[channels_of(*group[d])], sbuf.at[d], ssend.at[d], srecv.at[d], at(*group[d], z, core))
        for d in range(1, GROUP)
    ]
    for copy in s_copies:
        copy.start()

    for copy in g_copies + b_copies:
        copy.wait_recv()
    gs[...] = jnp.zeros_like(gs)
    part[...] = jnp.zeros_like(part)

    def pair(i, carry):
        for j in range(2):
            slot = 2 * i + j
            hot = onehot(vbuf[slot]).astype(BF16)
            ohs[:, EXT * j:EXT * (j + 1)] = jnp.concatenate([hot, hot, hot], axis=0)
            edge = jnp.zeros((SLICE, PAD), F32)
            wide = jnp.concatenate([edge, gbuf[slot].astype(F32), edge], axis=1)
            for k in range(KTAP):
                shift = (k - KTAP // 2) * DILATION_SECOND
                moved = wide if shift == 0 else pltpu.roll(wide, shift % EXT, 1)
                gs[SLICE * k:SLICE * (k + 1), EXT * j:EXT * (j + 1)] = moved.astype(BF16)
        hidden = jnp.dot(t3t[...], ohs[...], preferred_element_type=F32).astype(BF16)
        a2s[...] = jnp.maximum(hidden, 0)
        part[...] += lax.dot_general(a2s[...], gs[...], (((1,), (1,)), ((), ())), preferred_element_type=F32)
        return carry

    lax.fori_loop(0, GROUP // 2, pair, 0)

    def half_of(c):
        return pl.ds(pl.multiple_of(c * HALF, HALF), HALF)

    c_copy = remote(part.at[half_of(1 - core)], crecv, cs.at[0], cr.at[0], at(x, y, z, 1 - core))
    c_copy.start()
    for copy in s_copies:
        copy.wait_recv()
    group_sum = st[channels_of(x, y), :]
    for d in range(1, GROUP):
        group_sum = group_sum + sbuf[d]
    ssum[0] = group_sum
    sc_copy = remote(ssum.at[0], screcv, cs.at[1], cr.at[1], at(x, y, z, 1 - core))
    sc_copy.start()
    c_copy.wait_recv()
    part[half_of(core), :] += crecv[...]
    sc_copy.wait_recv()
    ssum[1] = ssum[0] + screcv[...]

    def z_rows(pz):
        return pl.ds(pl.multiple_of(core * HALF + pz * ZROWS, ZROWS), ZROWS)

    z_copies, sz_copies = [], []
    for d in range(1, NZ):
        pz = (z + d) % NZ
        z_copies.append(remote(part.at[z_rows(pz)], zrecv.at[d], zsend.at[d], zrsem.at[d], at(x, y, pz, core)))
        sz_copies.append(remote(ssum.at[1], szrecv.at[d], zsend.at[NZ + d], zrsem.at[NZ + d], at(x, y, pz, core)))
    for copy in z_copies + sz_copies:
        copy.start()

    for k in range(KTAP):
        start = PAD + (k - KTAP // 2) * DILATION_SECOND
        term = jnp.dot(a2f[start:start + ROWS, :].astype(BF16), w2[k], preferred_element_type=F32)
        acc[...] = term if k == 0 else acc[...] + term
    fvm[...] = (x1b[...].astype(F32) + acc[...]).astype(BF16)
    store = pltpu.make_async_copy(fvm, feat.at[0], lsem.at[1])
    store.start()

    for copy in z_copies + sz_copies:
        copy.wait_recv()
    total, s_total = part[z_rows(z), :], ssum[1]
    for d in range(1, NZ):
        total, s_total = total + zrecv[d], s_total + szrecv[d]
    zs[...] = total
    ssum[2] = s_total

    y_copies = []
    for d in range(1, NY):
        py = (y + d) % NY
        rows = pl.ds(pl.multiple_of(py * 8, 8), 8)
        y_copies.append(remote(zs.at[rows], yrecv.at[y], ys.at[d], yr.at[d], at(x, py, z, core)))
        y_copies.append(remote(ssum.at[2], syrecv.at[y], ys.at[NY + d], yr.at[NY + d], at(x, py, z, core)))
    for copy in y_copies:
        copy.start()
    yrecv[y] = zs[pl.ds(pl.multiple_of(y * 8, 8), 8), :]
    syrecv[y] = s_total
    for copy in y_copies:
        copy.wait_recv()

    lane = lax.broadcasted_iota(jnp.int32, (8, PAD), 1)
    by_base = jnp.concatenate([syrecv[i] for i in range(NY)], axis=0).T
    rows_act = a1t[pl.ds(pl.multiple_of(seq * 8, 8), 8), :]
    for k in range(KTAP):
        block = jnp.zeros((8, PAD), F32)
        for i in range(NY):
            piece = yrecv[i][:, PAD * (k // NY):PAD * (k // NY) + PAD]
            shift = (SLICE * (i - k % NY)) % PAD
            piece = piece if shift == 0 else pltpu.roll(piece, shift, 1)
            block = jnp.where((lane >= SLICE * i) & (lane < SLICE * (i + 1)), piece, block)
        out2[k] = block
        block = jnp.zeros((8, PAD), F32)
        for b in range(4):
            row = b * 16 + KTAP - 1 - k
            block = block + rows_act[:, b:b + 1] * by_base[row:row + 1, :]
        out1[k] = block

    store.wait()
    for copy in v_copies + h_copies + g_copies + b_copies + s_copies + [c_copy, sc_copy] + z_copies + sz_copies + y_copies:
        copy.wait_send()


def body(bases, gene, table, w1, w2, cotangent):
    vm = lambda *shape, dtype=F32: pltpu.VMEM(shape, dtype)
    dma = lambda n: pltpu.SemaphoreType.DMA((n,))
    vmem = pl.BlockSpec(memory_space=pltpu.VMEM)
    hbm = pl.BlockSpec(memory_space=pl.ANY)
    return pl.pallas_call(
        kernel,
        out_shape=(
            jax.ShapeDtypeStruct((1, ROWS, CH), BF16),
            jax.ShapeDtypeStruct((KTAP, 8, PAD), F32),
            jax.ShapeDtypeStruct((KTAP, 8, PAD), F32),
        ),
        in_specs=[vmem, vmem, vmem, hbm, hbm, hbm],
        out_specs=(hbm, vmem, vmem),
        scratch_shapes=[
            vm(KTAP, CH, CH, dtype=BF16),
            vm(KTAP, CH, CH, dtype=BF16),
            vm(EXT, CH, dtype=BF16),
            vm(EXT, CH),
            vm(CH, ROWS, dtype=BF16),
            vm(GROUP, SLICE, ROWS, dtype=BF16),
            vm(3, 8, ROWS),
            vm(GROUP, 8, PAD),
            vm(64, CH),
            vm(192, CH, dtype=BF16),
            vm(CH, 192, dtype=BF16),
            vm(CH, 16),
            vm(192, 2 * EXT, dtype=BF16),
            vm(ROWS, CH, dtype=BF16),
            vm(EXT, CH),
            vm(ROWS, CH),
            vm(ROWS, CH, dtype=BF16),
            vm(CH, PAD),
            vm(GROUP, SLICE, PAD),
            vm(CH, 2 * EXT, dtype=BF16),
            vm(WIDE, 2 * EXT, dtype=BF16),
            vm(CH, WIDE),
            vm(HALF, WIDE),
            vm(SLICE, PAD),
            vm(NZ, ZROWS, WIDE),
            vm(NZ, SLICE, PAD),
            vm(ZROWS, WIDE),
            vm(3, SLICE, PAD),
            vm(NY, 8, WIDE),
            vm(NY, SLICE, PAD),
            dma(KTAP), dma(KTAP), dma(2),
            dma(2), dma(2), dma(2), dma(2),
            dma(GROUP), dma(GROUP), dma(GROUP), dma(GROUP), dma(GROUP), dma(GROUP),
            dma(2), dma(2), dma(2 * NZ), dma(2 * NZ), dma(2 * NY), dma(2 * NY),
        ],
        compiler_params=pltpu.CompilerParams(
            collective_id=0, has_side_effects=True, vmem_limit_bytes=60 * 1024 * 1024
        ),
    )(bases, gene, table, cotangent, w1, w2)


def solution(mesh):
    return jax.shard_map(
        body,
        mesh=mesh,
        in_specs=(P("dp", "seq"), P("dp", "seq"), P(), P(), P(), P("dp", "seq", None)),
        out_specs=(P("dp", "seq", None), P(None, "seq", "dp"), P(None, "seq", "dp")),
        check_vma=False,
    )
```

```python
import jax
import jax.numpy as jnp
from jax import lax
from jax.experimental import pallas as pl
from jax.experimental.pallas import tpu as pltpu
from jax.sharding import PartitionSpec as P

MESH = pl.DeviceIdType.MESH
KTAP = 11
DILATION_FIRST = 4
DILATION_SECOND = 25
NX, NY, NZ, NC = 4, 4, 8, 2
SEQ = NY * NZ * NC
CH = 512
ROWS = 384
PAD = 128
EXT = ROWS + 2 * PAD
SLICE = CH // (NX * NY)
FOLD = SLICE // 2
WIDE = 384
GROUP = NX * NY
HALF = CH // NC
ZROWS = HALF // NZ
F32, BF16 = jnp.float32, jnp.bfloat16


def kernel(
    bases, gene, table, cot, w1_hbm, w2_hbm,
    feat, out1, out2,
    w1, w2, gvm, gf, gt, gbuf, vown, vbuf, tsc, t3, t3t, a1t, ohs, x1b, a2f, acc, fvm,
    st, sbuf, a2s, gs, turned_part, part, crecv, screcv, zout, zrecv, szrecv, zs, ssum, yrecv, syrecv,
    wsem, w2sem, lsem, hs, hr, vs, vr, gss, gsr, bs, br, ssend, srecv, cs, cr, zsend, zrsem, ys, yr,
):
    x = lax.axis_index("dp")
    seq = lax.axis_index("seq")
    core = seq % NC
    z = (seq // NC) % NZ
    y = seq // (NC * NZ)
    left, right = (seq + SEQ - 1) % SEQ, (seq + 1) % SEQ

    def at(px, py, pz, pc):
        return {"dp": px, "seq": (py * NZ + pz) * NC + pc}

    def remote(src, dst, ssem, rsem, device):
        return pltpu.make_async_remote_copy(
            src_ref=src, dst_ref=dst, send_sem=ssem, recv_sem=rsem, device_id=device, device_id_type=MESH
        )

    load_g = pltpu.make_async_copy(cot.at[0], gvm.at[pl.ds(PAD, ROWS)], lsem.at[0])
    load_g.start()
    load_w1 = [pltpu.make_async_copy(w1_hbm.at[k], w1.at[k], wsem.at[k]) for k in range(KTAP)]
    load_w2 = [pltpu.make_async_copy(w2_hbm.at[k], w2.at[k], w2sem.at[k]) for k in range(KTAP)]
    for copy in load_w1:
        copy.start()

    group = [((x + (0, 1, NX - 1, 2)[d // NY]) % NX, (y + d % NY) % NY) for d in range(GROUP)]
    partners = [{"dp": x, "seq": left}, {"dp": x, "seq": right}, at(x, y, z, 1 - core)]
    partners += [at(px, py, z, core) for px, py in group[1:]]
    partners += [at(x, y, (z + d) % NZ, core) for d in range(1, NZ)]
    barrier = pltpu.get_barrier_semaphore()
    for device in partners:
        pl.semaphore_signal(barrier, inc=1, device_id=device, device_id_type=MESH)

    label4 = 4.0 * gene[...].astype(F32)
    vown[1] = jnp.broadcast_to(bases[...].astype(F32) + label4, (8, ROWS))
    load_g.wait()
    own_g = gvm[PAD:PAD + ROWS, :]
    gt[...] = own_g.astype(F32).T.astype(BF16)
    pl.semaphore_wait(barrier, len(partners))

    v_copies = [
        remote(vown.at[1], vown.at[0], vs.at[0], vr.at[0], {"dp": x, "seq": right}),
        remote(vown.at[1], vown.at[2], vs.at[1], vr.at[1], {"dp": x, "seq": left}),
    ]
    h_copies = [
        remote(gvm.at[pl.ds(ROWS, PAD)], gvm.at[pl.ds(0, PAD)], hs.at[0], hr.at[0], {"dp": x, "seq": right}),
        remote(gvm.at[pl.ds(PAD, PAD)], gvm.at[pl.ds(PAD + ROWS, PAD)], hs.at[1], hr.at[1], {"dp": x, "seq": left}),
    ]

    def channels_of(px, py):
        return pl.ds(pl.multiple_of(px * (NY * SLICE) + py * SLICE, SLICE), SLICE)

    g_copies = [
        remote(gt.at[channels_of(*group[d])], gbuf.at[d], gss.at[d], gsr.at[d], at(*group[d], z, core))
        for d in range(1, GROUP)
    ]
    for copy in v_copies + h_copies + g_copies:
        copy.start()
    gbuf[0] = gt[channels_of(x, y), :]

    tab = table[...].astype(BF16).astype(F32)
    act = jnp.concatenate([jnp.maximum(tab, 0.0), jnp.zeros((12, CH), F32)], axis=0)
    a1t[...] = act.T
    act = act.astype(BF16)
    tsc[...] = jnp.zeros_like(tsc)
    for k in range(KTAP):
        load_w1[k].wait()
        load_w2[k].start()
        seen = jnp.dot(act, w1[k], preferred_element_type=F32)
        for b in range(4):
            row = seen[b:b + 1, :]
            if k == KTAP // 2:
                row = row + tab[b:b + 1, :]
            at_row = b * 16 + KTAP - 1 - k
            tsc[at_row:at_row + 1, :] = row
    whole = tsc[...]
    high = whole.astype(BF16).astype(F32)
    middle = (whole - high).astype(BF16).astype(F32)
    low = whole - high - middle
    thirds = jnp.concatenate([high, middle, low], axis=0)
    t3[...] = thirds.astype(BF16)
    t3t[...] = thirds.T.astype(BF16)

    for copy in v_copies:
        copy.wait_recv()
    v_left = jnp.where(seq == 0, -64.0, vown[0])
    v_right = jnp.where(seq == SEQ - 1, -64.0, vown[2])
    v_all = jnp.concatenate([v_left, vown[1], v_right], axis=1)
    ahead = PAD + 5 * DILATION_FIRST
    v_all = v_all[0:1, ahead:ahead + 7 * PAD]
    tiles = [v_all[:, PAD * r:PAD * (r + 1)] for r in range(7)]
    vbuf[0] = jnp.concatenate(tiles + [jnp.broadcast_to(label4, (1, PAD))], axis=0)
    b_copies = [
        remote(vbuf.at[0], vbuf.at[d], bs.at[d], br.at[d], at(*group[d], z, core)) for d in range(1, GROUP)
    ]
    for copy in b_copies:
        copy.start()

    def onehot(block):
        lanes = jnp.concatenate([block[r:r + 1, :] for r in range(7)], axis=1)
        own = block[7:8, 0:1]
        shifted = pltpu.roll(jnp.broadcast_to(lanes, (16, 7 * PAD)), 0, 1, stride=DILATION_FIRST, stride_axis=0)
        shifted = shifted[:, PAD:PAD + EXT]
        relative = shifted[5:6, :] - own
        own = jnp.where((relative >= 0.0) & (relative < 4.0), own, 1000.0)
        relative = shifted - own
        return jnp.concatenate([jnp.where(relative == float(b), 1.0, 0.0) for b in range(4)], axis=0)

    own_hot = onehot(vbuf[0])
    hot_rows = own_hot.T
    hot_rows = jnp.concatenate([hot_rows, hot_rows, hot_rows], axis=1).astype(BF16)
    x1 = jnp.dot(hot_rows, t3[...], preferred_element_type=F32).astype(BF16)
    x1b[...] = x1[PAD:PAD + ROWS, :]
    a2f[...] = jnp.maximum(x1.astype(F32), 0.0)

    for copy in h_copies:
        copy.wait_recv()
    keep_left = jnp.where(jnp.floor(v_left[0:1, 0:1] * 0.25) * 4.0 == label4, 1.0, 0.0)
    keep_right = jnp.where(jnp.floor(v_right[0:1, 0:1] * 0.25) * 4.0 == label4, 1.0, 0.0)
    gf[0:PAD, :] = gvm[0:PAD, :].astype(F32) * keep_left
    gf[PAD:PAD + ROWS, :] = own_g.astype(F32)
    gf[PAD + ROWS:, :] = gvm[PAD + ROWS:, :].astype(F32) * keep_right
    for copy in load_w2:
        copy.wait()
    for k in range(KTAP):
        start = PAD - (k - KTAP // 2) * DILATION_SECOND
        term = lax.dot_general(
            gf[start:start + ROWS, :].astype(BF16), w2[k], (((1,), (1,)), ((), ())), preferred_element_type=F32
        )
        acc[...] = term if k == 0 else acc[...] + term
    dx1 = (gf[PAD:PAD + ROWS, :] + jnp.where(x1b[...].astype(F32) > 0.0, acc[...], 0.0)).astype(BF16)
    sums = jnp.dot(own_hot[:, PAD:PAD + ROWS].astype(BF16), dx1, preferred_element_type=F32)
    first = (lax.broadcasted_iota(jnp.int32, sums.shape, 1) & FOLD) == 0
    sums = jnp.concatenate([jnp.where(first, sums, 0.0), jnp.where(first, 0.0, sums)], axis=0).T
    folded = [sums[i:i + FOLD, :] + sums[i + FOLD:i + SLICE, :] for i in range(0, CH, SLICE)]
    st[...] = jnp.concatenate(folded, axis=0)

    def folds_of(px, py):
        return pl.ds(pl.multiple_of((px * NY + py) * FOLD, FOLD), FOLD)

    s_copies = [
        remote(st.at[folds_of(*group[d])], sbuf.at[d], ssend.at[d], srecv.at[d], at(*group[d], z, core))
        for d in range(1, GROUP)
    ]
    for copy in s_copies:
        copy.start()

    gs[...] = jnp.zeros_like(gs)
    turned_part[...] = jnp.zeros_like(turned_part)
    middle_lanes, left_lanes = 2 * ROWS, 2 * (ROWS + PAD)

    def place(ref, rows, j, block, left_too=True, right_too=True):
        ref[rows, ROWS * j:ROWS * (j + 1)] = block[:, PAD:PAD + ROWS]
        if left_too:
            ref[rows, middle_lanes + PAD * j:middle_lanes + PAD * (j + 1)] = block[:, :PAD]
        if right_too:
            ref[rows, left_lanes + PAD * j:left_lanes + PAD * (j + 1)] = block[:, PAD + ROWS:]

    def pair(i, carry):
        for j in range(2):
            slot = 2 * i + j
            hot = onehot(vbuf[slot]).astype(BF16)
            place(ohs, slice(None), j, jnp.concatenate([hot, hot, hot], axis=0))
            edge = jnp.zeros((SLICE, PAD), F32)
            wide = jnp.concatenate([edge, gbuf[slot].astype(F32), edge], axis=1)
            for k in range(KTAP):
                offset = k - KTAP // 2
                moved = wide if offset == 0 else pltpu.roll(wide, (offset * DILATION_SECOND) % EXT, 1)
                place(gs, slice(SLICE * k, SLICE * (k + 1)), j, moved.astype(BF16), offset < 0, offset > 0)
        hidden = jnp.dot(t3t[...], ohs[...], preferred_element_type=F32)
        a2s[...] = jnp.maximum(hidden, 0.0).astype(BF16)
        before, after = SLICE * (KTAP // 2), SLICE * (KTAP // 2 + 1)
        for rows, lanes in (
            (slice(0, KTAP * SLICE), slice(0, middle_lanes)),
            (slice(0, before), slice(middle_lanes, left_lanes)),
            (slice(after, KTAP * SLICE), slice(left_lanes, 2 * EXT)),
        ):
            turned_part[rows, :] += lax.dot_general(
                gs[rows, lanes], a2s[:, lanes], (((1,), (1,)), ((), ())), preferred_element_type=F32
            )
        return carry

    def pairs(first, last):
        for d in range(max(1, 2 * first), 2 * last):
            g_copies[d - 1].wait_recv()
            b_copies[d - 1].wait_recv()
        lax.fori_loop(first, last, pair, 0)

    pairs(0, 2)
    pairs(2, 4)
    for copy in s_copies:
        copy.wait_recv()
    group_sum = st[folds_of(x, y), :]
    for d in range(1, GROUP):
        group_sum = group_sum + sbuf[d]
    ssum[0] = group_sum
    sc_copy = remote(ssum.at[0], screcv, cs.at[1], cr.at[1], at(x, y, z, 1 - core))
    sc_copy.start()
    pairs(4, 6)
    sc_copy.wait_recv()
    ssum[1] = ssum[0] + screcv[...]
    sz_copies = []
    for d in range(1, NZ):
        pz = (z + d) % NZ
        sz_copies.append(remote(ssum.at[1], szrecv.at[d], zsend.at[NZ + d], zrsem.at[NZ + d], at(x, y, pz, core)))
    for copy in sz_copies:
        copy.start()
    pairs(6, 8)
    turned = turned_part[...].T
    order = [(yy * NZ + zz) * NC + cc for cc in range(NC) for zz in range(NZ) for yy in range(NY)]
    part[...] = jnp.concatenate([turned[8 * s:8 * s + 8, :] for s in order], axis=0)

    def half_of(c):
        return pl.ds(pl.multiple_of(c * HALF, HALF), HALF)

    c_copy = remote(part.at[half_of(1 - core)], crecv, cs.at[0], cr.at[0], at(x, y, z, 1 - core))
    c_copy.start()
    for copy in sz_copies:
        copy.wait_recv()
    s_total = ssum[1]
    for d in range(1, NZ):
        s_total = s_total + szrecv[d]
    ssum[2] = s_total
    sy_copies = []
    for d in range(1, NY):
        py = (y + d) % NY
        sy_copies.append(remote(ssum.at[2], syrecv.at[y], ys.at[NY + d], yr.at[NY + d], at(x, py, z, core)))
    for copy in sy_copies:
        copy.start()
    syrecv[y] = s_total
    c_copy.wait_recv()
    own_half = part[half_of(core), :] + crecv[...]
    part[half_of(core), :] = own_half
    zout[...] = own_half.astype(BF16)

    z_copies = []
    for d in range(1, NZ):
        pz = (z + d) % NZ
        rows = pl.ds(pl.multiple_of(pz * ZROWS, ZROWS), ZROWS)
        z_copies.append(remote(zout.at[rows], zrecv.at[d], zsend.at[d], zrsem.at[d], at(x, y, pz, core)))
    for copy in z_copies:
        copy.start()

    for k in range(KTAP):
        start = PAD + (k - KTAP // 2) * DILATION_SECOND
        term = jnp.dot(a2f[start:start + ROWS, :].astype(BF16), w2[k], preferred_element_type=F32)
        acc[...] = term if k == 0 else acc[...] + term
    fvm[...] = (x1b[...].astype(F32) + acc[...]).astype(BF16)
    store = pltpu.make_async_copy(fvm, feat.at[0], lsem.at[1])
    store.start()

    for copy in z_copies:
        copy.wait_recv()
    total = part[pl.ds(pl.multiple_of(core * HALF + z * ZROWS, ZROWS), ZROWS), :]
    for d in range(1, NZ):
        total = total + zrecv[d].astype(F32)
    zs[...] = total

    y_copies = []
    for d in range(1, NY):
        py = (y + d) % NY
        rows = pl.ds(pl.multiple_of(py * 8, 8), 8)
        y_copies.append(remote(zs.at[rows], yrecv.at[y], ys.at[d], yr.at[d], at(x, py, z, core)))
    for copy in y_copies:
        copy.start()
    yrecv[y] = zs[pl.ds(pl.multiple_of(y * 8, 8), 8), :]
    for copy in y_copies + sy_copies:
        copy.wait_recv()

    lane = lax.broadcasted_iota(jnp.int32, (8, PAD), 1)
    unfolded = [side for i in range(NY) for side in (syrecv[i], pltpu.roll(syrecv[i], PAD // 2, 1))]
    by_base = jnp.concatenate(unfolded, axis=0).T
    rows_act = a1t[pl.ds(pl.multiple_of(seq * 8, 8), 8), :]
    for k in range(KTAP):
        block = jnp.zeros((8, PAD), F32)
        for i in range(NY):
            piece = yrecv[i][:, PAD * (k // NY):PAD * (k // NY) + PAD]
            shift = (SLICE * (i - k % NY)) % PAD
            piece = piece if shift == 0 else pltpu.roll(piece, shift, 1)
            block = jnp.where((lane >= SLICE * i) & (lane < SLICE * (i + 1)), piece, block)
        out2[k] = block
        block = jnp.zeros((8, PAD), F32)
        for b in range(4):
            row = b * 16 + KTAP - 1 - k
            block = block + rows_act[:, b:b + 1] * by_base[row:row + 1, :]
        out1[k] = block

    store.wait()
    sent = v_copies + h_copies + g_copies + b_copies + s_copies + [c_copy, sc_copy]
    for copy in sent + z_copies + sz_copies + y_copies + sy_copies:
        copy.wait_send()


def hand_over(feat, grad1, grad2, feat_out, out1, out2):
    feat_out[...] = feat[...]
    out1[...] = grad1[...]
    out2[...] = grad2[...]


def body(bases, gene, table, w1, w2, cotangent):
    vm = lambda *shape, dtype=F32: pltpu.VMEM(shape, dtype)
    dma = lambda n: pltpu.SemaphoreType.DMA((n,))
    vmem = pl.BlockSpec(memory_space=pltpu.VMEM)
    hbm = pl.BlockSpec(memory_space=pl.ANY)
    outs = (
        jax.ShapeDtypeStruct((1, ROWS, CH), BF16),
        jax.ShapeDtypeStruct((KTAP, 8, PAD), F32),
        jax.ShapeDtypeStruct((KTAP, 8, PAD), F32),
    )
    results = pl.pallas_call(
        kernel,
        out_shape=outs,
        in_specs=[vmem, vmem, vmem, hbm, hbm, hbm],
        out_specs=(hbm, vmem, vmem),
        scratch_shapes=[
            vm(KTAP, CH, CH, dtype=BF16),
            vm(KTAP, CH, CH, dtype=BF16),
            vm(EXT, CH, dtype=BF16),
            vm(EXT, CH),
            vm(CH, ROWS, dtype=BF16),
            vm(GROUP, SLICE, ROWS, dtype=BF16),
            vm(3, 8, ROWS),
            vm(GROUP, 8, PAD),
            vm(64, CH),
            vm(192, CH, dtype=BF16),
            vm(CH, 192, dtype=BF16),
            vm(CH, 16),
            vm(192, 2 * EXT, dtype=BF16),
            vm(ROWS, CH, dtype=BF16),
            vm(EXT, CH),
            vm(ROWS, CH),
            vm(ROWS, CH, dtype=BF16),
            vm(CH // 2, PAD),
            vm(GROUP, FOLD, PAD),
            vm(CH, 2 * EXT, dtype=BF16),
            vm(WIDE, 2 * EXT, dtype=BF16),
            vm(WIDE, CH),
            vm(CH, WIDE),
            vm(HALF, WIDE),
            vm(FOLD, PAD),
            vm(HALF, WIDE, dtype=BF16),
            vm(NZ, ZROWS, WIDE, dtype=BF16),
            vm(NZ, FOLD, PAD),
            vm(ZROWS, WIDE),
            vm(3, FOLD, PAD),
            vm(NY, 8, WIDE),
            vm(NY, FOLD, PAD),
            dma(KTAP), dma(KTAP), dma(2),
            dma(2), dma(2), dma(2), dma(2),
            dma(GROUP), dma(GROUP), dma(GROUP), dma(GROUP), dma(GROUP), dma(GROUP),
            dma(2), dma(2), dma(2 * NZ), dma(2 * NZ), dma(2 * NY), dma(2 * NY),
        ],
        compiler_params=pltpu.CompilerParams(
            collective_id=0, has_side_effects=True, vmem_limit_bytes=60 * 1024 * 1024
        ),
    )(bases, gene, table, cotangent, w1, w2)
    return pl.pallas_call(
        hand_over,
        out_shape=outs,
        in_specs=[vmem, vmem, vmem],
        out_specs=(vmem, vmem, vmem),
    )(*results)


def solution(mesh):
    return jax.shard_map(
        body,
        mesh=mesh,
        in_specs=(P("dp", "seq"), P("dp", "seq"), P(), P(), P(), P("dp", "seq", None)),
        out_specs=(P("dp", "seq", None), P(None, "seq", "dp"), P(None, "seq", "dp")),
        check_vma=False,
    )
```

```python
import jax
import jax.numpy as jnp
from jax import lax
from jax.experimental import pallas as pl
from jax.experimental.pallas import tpu as pltpu
from jax.sharding import PartitionSpec as P

MESH = pl.DeviceIdType.MESH
KTAP = 11
DILATION_FIRST = 4
DILATION_SECOND = 25
NX, NY, NZ, NC = 4, 4, 8, 2
SEQ = NY * NZ * NC
CH = 512
ROWS = 384
PAD = 128
EXT = ROWS + 2 * PAD
SLICE = CH // (NX * NY)
FOLD = SLICE // 2
WIDE = 384
GROUP = NX * NY
HALF = CH // NC
ZROWS = HALF // NZ
SHARE = (KTAP + 1) // NC
F32, BF16 = jnp.float32, jnp.bfloat16


def kernel(
    bases_in, gene_in, table_in, cot, w1_hbm, w2_hbm,
    feat, out1, out2,
    bases, gene, table, w1, w2, tmine, tother, gvm, gf, gt, gbuf, vown, vbuf, tsc, t3, t3t, a1t, ohs, x1b, a2f, acc, fvm,
    st, sbuf, a2s, gs, turned_part, part, crecv, screcv, zout, zrecv, szrecv, zs, ssum, yrecv, syrecv,
    wsem, w2sem, lsem, ts, tr, hs, hr, vs, vr, gss, gsr, bs, br, ssend, srecv, cs, cr, zsend, zrsem, ys, yr,
):
    x = lax.axis_index("dp")
    seq = lax.axis_index("seq")
    core = seq % NC
    z = (seq // NC) % NZ
    y = seq // (NC * NZ)
    left, right = (seq + SEQ - 1) % SEQ, (seq + 1) % SEQ

    def at(px, py, pz, pc):
        return {"dp": px, "seq": (py * NZ + pz) * NC + pc}

    def remote(src, dst, ssem, rsem, device):
        return pltpu.make_async_remote_copy(
            src_ref=src, dst_ref=dst, send_sem=ssem, recv_sem=rsem, device_id=device, device_id_type=MESH
        )

    group = [((x + (0, 1, NX - 1, 2)[d // NY]) % NX, (y + d % NY) % NY) for d in range(GROUP)]
    partners = [{"dp": x, "seq": left}, {"dp": x, "seq": right}, at(x, y, z, 1 - core)]
    partners += [at(px, py, z, core) for px, py in group[1:]]
    partners += [at(x, y, (z + d) % NZ, core) for d in range(1, NZ)]
    barrier = pltpu.get_barrier_semaphore()
    for device in partners:
        pl.semaphore_signal(barrier, inc=1, device_id=device, device_id_type=MESH)

    small = [
        pltpu.make_async_copy(src, dst, lsem.at[2 + i])
        for i, (src, dst) in enumerate(((bases_in, bases), (gene_in, gene), (table_in, table)))
    ]
    load_g = pltpu.make_async_copy(cot.at[0], gvm.at[pl.ds(PAD, ROWS)], lsem.at[0])
    load_w1 = [pltpu.make_async_copy(w1_hbm.at[core * (SHARE - 1) + i], w1.at[i], wsem.at[i]) for i in range(SHARE)]
    load_w2 = [pltpu.make_async_copy(w2_hbm.at[k], w2.at[k], w2sem.at[k]) for k in range(KTAP)]
    for copy in small + [load_g] + load_w1:
        copy.start()

    for copy in small:
        copy.wait()
    label4 = 4.0 * gene[...].astype(F32)
    vown[1] = jnp.broadcast_to(bases[...].astype(F32) + label4, (8, ROWS))
    load_g.wait()
    own_g = gvm[PAD:PAD + ROWS, :]
    gt[...] = own_g.astype(F32).T.astype(BF16)
    pl.semaphore_wait(barrier, len(partners))

    v_copies = [
        remote(vown.at[1], vown.at[0], vs.at[0], vr.at[0], {"dp": x, "seq": right}),
        remote(vown.at[1], vown.at[2], vs.at[1], vr.at[1], {"dp": x, "seq": left}),
    ]
    h_copies = [
        remote(gvm.at[pl.ds(ROWS, PAD)], gvm.at[pl.ds(0, PAD)], hs.at[0], hr.at[0], {"dp": x, "seq": right}),
        remote(gvm.at[pl.ds(PAD, PAD)], gvm.at[pl.ds(PAD + ROWS, PAD)], hs.at[1], hr.at[1], {"dp": x, "seq": left}),
    ]

    def channels_of(px, py):
        return pl.ds(pl.multiple_of(px * (NY * SLICE) + py * SLICE, SLICE), SLICE)

    g_copies = [
        remote(gt.at[channels_of(*group[d])], gbuf.at[d], gss.at[d], gsr.at[d], at(*group[d], z, core))
        for d in range(1, GROUP)
    ]
    for copy in v_copies + h_copies + g_copies:
        copy.start()
    gbuf[0] = gt[channels_of(x, y), :]

    tab = table[...].astype(BF16).astype(F32)
    act = jnp.concatenate([jnp.maximum(tab, 0.0), jnp.zeros((12, CH), F32)], axis=0)
    a1t[...] = act.T
    act = act.astype(BF16)
    for i in range(SHARE):
        load_w1[i].wait()
        for copy in load_w2[2 * i:2 * i + 2]:
            copy.start()
        tmine[i] = jnp.dot(act, w1[i], preferred_element_type=F32)[0:8, :]
    t_copy = remote(tmine, tother, ts.at[0], tr.at[0], at(x, y, z, 1 - core))
    t_copy.start()

    for copy in v_copies:
        copy.wait_recv()
    v_left = jnp.where(seq == 0, -64.0, vown[0])
    v_right = jnp.where(seq == SEQ - 1, -64.0, vown[2])
    v_all = jnp.concatenate([v_left, vown[1], v_right], axis=1)
    ahead = PAD + 5 * DILATION_FIRST
    v_all = v_all[0:1, ahead:ahead + 7 * PAD]
    tiles = [v_all[:, PAD * r:PAD * (r + 1)] for r in range(7)]
    vbuf[0] = jnp.concatenate(tiles + [jnp.broadcast_to(label4, (1, PAD))], axis=0)
    b_copies = [
        remote(vbuf.at[0], vbuf.at[d], bs.at[d], br.at[d], at(*group[d], z, core)) for d in range(1, GROUP)
    ]
    for copy in b_copies:
        copy.start()

    def onehot(block):
        lanes = jnp.concatenate([block[r:r + 1, :] for r in range(7)], axis=1)
        own = block[7:8, 0:1]
        shifted = pltpu.roll(jnp.broadcast_to(lanes, (16, 7 * PAD)), 0, 1, stride=DILATION_FIRST, stride_axis=0)
        shifted = shifted[:, PAD:PAD + EXT]
        relative = shifted[5:6, :] - own
        own = jnp.where((relative >= 0.0) & (relative < 4.0), own, 1000.0)
        relative = shifted - own
        return jnp.concatenate([jnp.where(relative == float(b), 1.0, 0.0) for b in range(4)], axis=0)

    for copy in h_copies:
        copy.wait_recv()
    keep_left = jnp.where(jnp.floor(v_left[0:1, 0:1] * 0.25) * 4.0 == label4, 1.0, 0.0)
    keep_right = jnp.where(jnp.floor(v_right[0:1, 0:1] * 0.25) * 4.0 == label4, 1.0, 0.0)
    gf[0:PAD, :] = gvm[0:PAD, :].astype(F32) * keep_left
    gf[PAD:PAD + ROWS, :] = own_g.astype(F32)
    gf[PAD + ROWS:, :] = gvm[PAD + ROWS:, :].astype(F32) * keep_right
    for k in range(KTAP):
        load_w2[k].wait()
        start = PAD - (k - KTAP // 2) * DILATION_SECOND
        term = lax.dot_general(
            gf[start:start + ROWS, :].astype(BF16), w2[k], (((1,), (1,)), ((), ())), preferred_element_type=F32
        )
        acc[...] = term if k == 0 else acc[...] + term
    t_copy.wait_recv()
    tsc[...] = jnp.zeros_like(tsc)
    for k in range(KTAP):
        i = k if k < SHARE else k - SHARE + 1
        seen = jnp.where(core == (0 if k < SHARE else 1), tmine[i], tother[i])
        for b in range(4):
            row = seen[b:b + 1, :]
            if k == KTAP // 2:
                row = row + tab[b:b + 1, :]
            at_row = b * 16 + KTAP - 1 - k
            tsc[at_row:at_row + 1, :] = row
    whole = tsc[...]
    high = whole.astype(BF16).astype(F32)
    middle = (whole - high).astype(BF16).astype(F32)
    low = whole - high - middle
    thirds = jnp.concatenate([high, middle, low], axis=0)
    t3[...] = thirds.astype(BF16)
    t3t[...] = thirds.T.astype(BF16)

    own_hot = onehot(vbuf[0])
    hot_rows = own_hot.T
    hot_rows = jnp.concatenate([hot_rows, hot_rows, hot_rows], axis=1).astype(BF16)
    x1 = jnp.dot(hot_rows, t3[...], preferred_element_type=F32).astype(BF16)
    x1b[...] = x1[PAD:PAD + ROWS, :]
    a2f[...] = jnp.maximum(x1.astype(F32), 0.0)

    dx1 = (gf[PAD:PAD + ROWS, :] + jnp.where(x1b[...].astype(F32) > 0.0, acc[...], 0.0)).astype(BF16)
    sums = jnp.dot(own_hot[:, PAD:PAD + ROWS].astype(BF16), dx1, preferred_element_type=F32)
    first = (lax.broadcasted_iota(jnp.int32, sums.shape, 1) & FOLD) == 0
    sums = jnp.concatenate([jnp.where(first, sums, 0.0), jnp.where(first, 0.0, sums)], axis=0).T
    folded = [sums[i:i + FOLD, :] + sums[i + FOLD:i + SLICE, :] for i in range(0, CH, SLICE)]
    st[...] = jnp.concatenate(folded, axis=0)

    def folds_of(px, py):
        return pl.ds(pl.multiple_of((px * NY + py) * FOLD, FOLD), FOLD)

    s_copies = [
        remote(st.at[folds_of(*group[d])], sbuf.at[d], ssend.at[d], srecv.at[d], at(*group[d], z, core))
        for d in range(1, GROUP)
    ]
    for copy in s_copies:
        copy.start()

    gs[...] = jnp.zeros_like(gs)
    turned_part[...] = jnp.zeros_like(turned_part)
    middle_lanes, left_lanes = 2 * ROWS, 2 * (ROWS + PAD)

    def place(ref, rows, j, block, left_too=True, right_too=True):
        ref[rows, ROWS * j:ROWS * (j + 1)] = block[:, PAD:PAD + ROWS]
        if left_too:
            ref[rows, middle_lanes + PAD * j:middle_lanes + PAD * (j + 1)] = block[:, :PAD]
        if right_too:
            ref[rows, left_lanes + PAD * j:left_lanes + PAD * (j + 1)] = block[:, PAD + ROWS:]

    def pair(i, carry):
        for j in range(2):
            slot = 2 * i + j
            hot = onehot(vbuf[slot]).astype(BF16)
            place(ohs, slice(None), j, jnp.concatenate([hot, hot, hot], axis=0))
            edge = jnp.zeros((SLICE, PAD), F32)
            wide = jnp.concatenate([edge, gbuf[slot].astype(F32), edge], axis=1)
            for k in range(KTAP):
                offset = k - KTAP // 2
                moved = wide if offset == 0 else pltpu.roll(wide, (offset * DILATION_SECOND) % EXT, 1)
                place(gs, slice(SLICE * k, SLICE * (k + 1)), j, moved.astype(BF16), offset < 0, offset > 0)
        hidden = jnp.dot(t3t[...], ohs[...], preferred_element_type=F32)
        a2s[...] = jnp.maximum(hidden, 0.0).astype(BF16)
        before, after = SLICE * (KTAP // 2), SLICE * (KTAP // 2 + 1)
        for rows, lanes in (
            (slice(0, KTAP * SLICE), slice(0, middle_lanes)),
            (slice(0, before), slice(middle_lanes, left_lanes)),
            (slice(after, KTAP * SLICE), slice(left_lanes, 2 * EXT)),
        ):
            turned_part[rows, :] += lax.dot_general(
                gs[rows, lanes], a2s[:, lanes], (((1,), (1,)), ((), ())), preferred_element_type=F32
            )
        return carry

    def pairs(first, last):
        for d in range(max(1, 2 * first), 2 * last):
            g_copies[d - 1].wait_recv()
            b_copies[d - 1].wait_recv()
        lax.fori_loop(first, last, pair, 0)

    pairs(0, 2)
    pairs(2, 4)
    pairs(4, 6)
    for copy in s_copies:
        copy.wait_recv()
    group_sum = st[folds_of(x, y), :]
    for d in range(1, GROUP):
        group_sum = group_sum + sbuf[d]
    ssum[0] = group_sum
    sc_copy = remote(ssum.at[0], screcv, cs.at[1], cr.at[1], at(x, y, z, 1 - core))
    sc_copy.start()
    pairs(6, 7)
    sc_copy.wait_recv()
    ssum[1] = ssum[0] + screcv[...]
    sz_copies = []
    for d in range(1, NZ):
        pz = (z + d) % NZ
        sz_copies.append(remote(ssum.at[1], szrecv.at[d], zsend.at[NZ + d], zrsem.at[NZ + d], at(x, y, pz, core)))
    for copy in sz_copies:
        copy.start()
    pairs(7, 8)
    turned = turned_part[...].T
    order = [(yy * NZ + zz) * NC + cc for cc in range(NC) for zz in range(NZ) for yy in range(NY)]
    part[...] = jnp.concatenate([turned[8 * s:8 * s + 8, :] for s in order], axis=0)

    def half_of(c):
        return pl.ds(pl.multiple_of(c * HALF, HALF), HALF)

    c_copy = remote(part.at[half_of(1 - core)], crecv, cs.at[0], cr.at[0], at(x, y, z, 1 - core))
    c_copy.start()
    c_copy.wait_recv()
    own_half = part[half_of(core), :] + crecv[...]
    part[half_of(core), :] = own_half
    zout[...] = own_half.astype(BF16)

    z_copies = []
    for d in range(1, NZ):
        pz = (z + d) % NZ
        rows = pl.ds(pl.multiple_of(pz * ZROWS, ZROWS), ZROWS)
        z_copies.append(remote(zout.at[rows], zrecv.at[d], zsend.at[d], zrsem.at[d], at(x, y, pz, core)))
    for copy in z_copies:
        copy.start()

    for k in range(KTAP):
        start = PAD + (k - KTAP // 2) * DILATION_SECOND
        term = jnp.dot(a2f[start:start + ROWS, :].astype(BF16), w2[k], preferred_element_type=F32)
        acc[...] = term if k == 0 else acc[...] + term
    fvm[...] = (x1b[...].astype(F32) + acc[...]).astype(BF16)
    store = pltpu.make_async_copy(fvm, feat.at[0], lsem.at[1])
    store.start()

    for copy in sz_copies:
        copy.wait_recv()
    s_total = ssum[1]
    for d in range(1, NZ):
        s_total = s_total + szrecv[d]
    ssum[2] = s_total
    sy_copies = []
    for d in range(1, NY):
        py = (y + d) % NY
        sy_copies.append(remote(ssum.at[2], syrecv.at[y], ys.at[NY + d], yr.at[NY + d], at(x, py, z, core)))
    for copy in sy_copies:
        copy.start()
    syrecv[y] = s_total
    for copy in z_copies:
        copy.wait_recv()
    total = part[pl.ds(pl.multiple_of(core * HALF + z * ZROWS, ZROWS), ZROWS), :]
    for d in range(1, NZ):
        total = total + zrecv[d].astype(F32)
    zs[...] = total


    y_copies = []
    for d in range(1, NY):
        py = (y + d) % NY
        rows = pl.ds(pl.multiple_of(py * 8, 8), 8)
        y_copies.append(remote(zs.at[rows], yrecv.at[y], ys.at[d], yr.at[d], at(x, py, z, core)))
    for copy in y_copies:
        copy.start()
    yrecv[y] = zs[pl.ds(pl.multiple_of(y * 8, 8), 8), :]
    for copy in y_copies + sy_copies:
        copy.wait_recv()

    lane = lax.broadcasted_iota(jnp.int32, (8, PAD), 1)
    unfolded = [side for i in range(NY) for side in (syrecv[i], pltpu.roll(syrecv[i], PAD // 2, 1))]
    by_base = jnp.concatenate(unfolded, axis=0).T
    rows_act = a1t[pl.ds(pl.multiple_of(seq * 8, 8), 8), :]
    for k in range(KTAP):
        block = jnp.zeros((8, PAD), F32)
        for i in range(NY):
            piece = yrecv[i][:, PAD * (k // NY):PAD * (k // NY) + PAD]
            shift = (SLICE * (i - k % NY)) % PAD
            piece = piece if shift == 0 else pltpu.roll(piece, shift, 1)
            block = jnp.where((lane >= SLICE * i) & (lane < SLICE * (i + 1)), piece, block)
        out2[k] = block
        block = jnp.zeros((8, PAD), F32)
        for b in range(4):
            row = b * 16 + KTAP - 1 - k
            block = block + rows_act[:, b:b + 1] * by_base[row:row + 1, :]
        out1[k] = block

    store.wait()
    sent = v_copies + h_copies + g_copies + b_copies + s_copies + [t_copy, c_copy, sc_copy]
    for copy in sent + z_copies + sz_copies + y_copies + sy_copies:
        copy.wait_send()


def hand_over(feat, grad1, grad2, feat_out, out1, out2):
    feat_out[...] = feat[...]
    out1[...] = grad1[...]
    out2[...] = grad2[...]


def body(bases, gene, table, w1, w2, cotangent):
    vm = lambda *shape, dtype=F32: pltpu.VMEM(shape, dtype)
    dma = lambda n: pltpu.SemaphoreType.DMA((n,))
    vmem = pl.BlockSpec(memory_space=pltpu.VMEM)
    hbm = pl.BlockSpec(memory_space=pl.ANY)
    outs = (
        jax.ShapeDtypeStruct((1, ROWS, CH), BF16),
        jax.ShapeDtypeStruct((KTAP, 8, PAD), F32),
        jax.ShapeDtypeStruct((KTAP, 8, PAD), F32),
    )
    results = pl.pallas_call(
        kernel,
        out_shape=outs,
        in_specs=[hbm] * 6,
        out_specs=(hbm, vmem, vmem),
        scratch_shapes=[
            vm(1, ROWS, dtype=jnp.int32),
            vm(1, 1, dtype=jnp.int32),
            vm(4, CH),
            vm(SHARE, CH, CH, dtype=BF16),
            vm(KTAP, CH, CH, dtype=BF16),
            vm(SHARE, 8, CH),
            vm(SHARE, 8, CH),
            vm(EXT, CH, dtype=BF16),
            vm(EXT, CH),
            vm(CH, ROWS, dtype=BF16),
            vm(GROUP, SLICE, ROWS, dtype=BF16),
            vm(3, 8, ROWS),
            vm(GROUP, 8, PAD),
            vm(64, CH),
            vm(192, CH, dtype=BF16),
            vm(CH, 192, dtype=BF16),
            vm(CH, 16),
            vm(192, 2 * EXT, dtype=BF16),
            vm(ROWS, CH, dtype=BF16),
            vm(EXT, CH),
            vm(ROWS, CH),
            vm(ROWS, CH, dtype=BF16),
            vm(CH // 2, PAD),
            vm(GROUP, FOLD, PAD),
            vm(CH, 2 * EXT, dtype=BF16),
            vm(WIDE, 2 * EXT, dtype=BF16),
            vm(WIDE, CH),
            vm(CH, WIDE),
            vm(HALF, WIDE),
            vm(FOLD, PAD),
            vm(HALF, WIDE, dtype=BF16),
            vm(NZ, ZROWS, WIDE, dtype=BF16),
            vm(NZ, FOLD, PAD),
            vm(ZROWS, WIDE),
            vm(3, FOLD, PAD),
            vm(NY, 8, WIDE),
            vm(NY, FOLD, PAD),
            dma(SHARE), dma(KTAP), dma(5), dma(1), dma(1),
            dma(2), dma(2), dma(2), dma(2),
            dma(GROUP), dma(GROUP), dma(GROUP), dma(GROUP), dma(GROUP), dma(GROUP),
            dma(2), dma(2), dma(2 * NZ), dma(2 * NZ), dma(2 * NY), dma(2 * NY),
        ],
        compiler_params=pltpu.CompilerParams(
            collective_id=0, has_side_effects=True, vmem_limit_bytes=60 * 1024 * 1024
        ),
    )(bases, gene, table, cotangent, w1, w2)
    return pl.pallas_call(
        hand_over,
        out_shape=outs,
        in_specs=[vmem, vmem, vmem],
        out_specs=(vmem, vmem, vmem),
    )(*results)


def solution(mesh):
    return jax.shard_map(
        body,
        mesh=mesh,
        in_specs=(P("dp", "seq"), P("dp", "seq"), P(), P(), P(), P("dp", "seq", None)),
        out_specs=(P("dp", "seq", None), P(None, "seq", "dp"), P(None, "seq", "dp")),
        check_vma=False,
    )
```

```python
import jax
import jax.numpy as jnp
from jax import lax
from jax.experimental import pallas as pl
from jax.experimental.pallas import tpu as pltpu
from jax.sharding import PartitionSpec as P

MESH = pl.DeviceIdType.MESH
KTAP = 11
DILATION_FIRST = 4
DILATION_SECOND = 25
NX, NY, NZ, NC = 4, 4, 8, 2
SEQ = NY * NZ * NC
CH = 512
ROWS = 384
PAD = 128
EXT = ROWS + 2 * PAD
SLICE = CH // (NX * NY)
FOLD = SLICE // 2
WIDE = 384
GROUP = NX * NY
HALF = CH // NC
ZROWS = HALF // NZ
SHARE = (KTAP + 1) // NC
F32, BF16 = jnp.float32, jnp.bfloat16


def kernel(
    bases_in, gene_in, table_in, cot, w1_hbm, w2_hbm,
    feat, out1, out2,
    bases, gene, table, w1, w2, tmine, tother, gvm, gf, gt, gbuf, vown, vbuf, tsc, t3, t3t, a1t, ohs, x1b, a2f, acc, fvm,
    st, sbuf, a2s, gs, turned_part, part, crecv, screcv, zout, zrecv, szrecv, zs, ssum, yrecv, syrecv,
    wsem, w2sem, lsem, ts, tr, hs, hr, vs, vr, gss, gsr, bs, br, ssend, srecv, cs, cr, zsend, zrsem, ys, yr,
):
    x = lax.axis_index("dp")
    seq = lax.axis_index("seq")
    core = seq % NC
    z = (seq // NC) % NZ
    y = seq // (NC * NZ)
    left, right = (seq + SEQ - 1) % SEQ, (seq + 1) % SEQ

    def at(px, py, pz, pc):
        return {"dp": px, "seq": (py * NZ + pz) * NC + pc}

    def remote(src, dst, ssem, rsem, device):
        return pltpu.make_async_remote_copy(
            src_ref=src, dst_ref=dst, send_sem=ssem, recv_sem=rsem, device_id=device, device_id_type=MESH
        )

    group = [((x + (0, 1, NX - 1, 2)[d // NY]) % NX, (y + d % NY) % NY) for d in range(GROUP)]
    partners = [{"dp": x, "seq": left}, {"dp": x, "seq": right}, at(x, y, z, 1 - core)]
    partners += [at(px, py, z, core) for px, py in group[1:]]
    partners += [at(x, y, (z + d) % NZ, core) for d in range(1, NZ)]
    barrier = pltpu.get_barrier_semaphore()
    for device in partners:
        pl.semaphore_signal(barrier, inc=1, device_id=device, device_id_type=MESH)

    small = [
        pltpu.make_async_copy(src, dst, lsem.at[2 + i])
        for i, (src, dst) in enumerate(((bases_in, bases), (gene_in, gene), (table_in, table)))
    ]
    load_g = pltpu.make_async_copy(cot.at[0], gvm.at[pl.ds(PAD, ROWS)], lsem.at[0])
    load_w1 = [pltpu.make_async_copy(w1_hbm.at[core * (SHARE - 1) + i], w1.at[i], wsem.at[i]) for i in range(SHARE)]
    load_w2 = [pltpu.make_async_copy(w2_hbm.at[k], w2.at[k], w2sem.at[k]) for k in range(KTAP)]
    for copy in small + [load_g] + load_w1:
        copy.start()

    for copy in small:
        copy.wait()
    label4 = 4.0 * gene[...].astype(F32)
    vown[1] = jnp.broadcast_to(bases[...].astype(F32) + label4, (8, ROWS))
    load_g.wait()
    own_g = gvm[PAD:PAD + ROWS, :]
    gt[...] = own_g.astype(F32).T.astype(BF16)
    pl.semaphore_wait(barrier, len(partners))

    v_copies = [
        remote(vown.at[1], vown.at[0], vs.at[0], vr.at[0], {"dp": x, "seq": right}),
        remote(vown.at[1], vown.at[2], vs.at[1], vr.at[1], {"dp": x, "seq": left}),
    ]
    h_copies = [
        remote(gvm.at[pl.ds(ROWS, PAD)], gvm.at[pl.ds(0, PAD)], hs.at[0], hr.at[0], {"dp": x, "seq": right}),
        remote(gvm.at[pl.ds(PAD, PAD)], gvm.at[pl.ds(PAD + ROWS, PAD)], hs.at[1], hr.at[1], {"dp": x, "seq": left}),
    ]

    def channels_of(px, py):
        return pl.ds(pl.multiple_of(px * (NY * SLICE) + py * SLICE, SLICE), SLICE)

    g_copies = [
        remote(gt.at[channels_of(*group[d])], gbuf.at[d], gss.at[d], gsr.at[d], at(*group[d], z, core))
        for d in range(1, GROUP)
    ]
    for copy in v_copies + h_copies:
        copy.start()
    gbuf[0] = gt[channels_of(x, y), :]

    tab = table[...].astype(BF16).astype(F32)
    act = jnp.concatenate([jnp.maximum(tab, 0.0), jnp.zeros((12, CH), F32)], axis=0)
    a1t[...] = act.T
    act = act.astype(BF16)
    def share(i):
        load_w1[i].wait()
        for copy in load_w2[2 * i:2 * i + 2]:
            copy.start()
        tmine[i] = jnp.dot(act, w1[i], preferred_element_type=F32)[0:8, :]
        if i == 0:
            for copy in g_copies:
                copy.start()

    share(0)
    share(1)

    for copy in v_copies:
        copy.wait_recv()
    v_left = jnp.where(seq == 0, -64.0, vown[0])
    v_right = jnp.where(seq == SEQ - 1, -64.0, vown[2])
    v_all = jnp.concatenate([v_left, vown[1], v_right], axis=1)
    ahead = PAD + 5 * DILATION_FIRST
    v_all = v_all[0:1, ahead:ahead + 7 * PAD]
    tiles = [v_all[:, PAD * r:PAD * (r + 1)] for r in range(7)]
    vbuf[0] = jnp.concatenate(tiles + [jnp.broadcast_to(label4, (1, PAD))], axis=0)
    b_copies = [
        remote(vbuf.at[0], vbuf.at[d], bs.at[d], br.at[d], at(*group[d], z, core)) for d in range(1, GROUP)
    ]
    for copy in b_copies:
        copy.start()

    for i in range(2, SHARE):
        share(i)
    t_copy = remote(tmine, tother, ts.at[0], tr.at[0], at(x, y, z, 1 - core))
    t_copy.start()

    def onehot(block):
        lanes = jnp.concatenate([block[r:r + 1, :] for r in range(7)], axis=1)
        own = block[7:8, 0:1]
        shifted = pltpu.roll(jnp.broadcast_to(lanes, (16, 7 * PAD)), 0, 1, stride=DILATION_FIRST, stride_axis=0)
        shifted = shifted[:, PAD:PAD + EXT]
        relative = shifted[5:6, :] - own
        own = jnp.where((relative >= 0.0) & (relative < 4.0), own, 1000.0)
        relative = shifted - own
        return jnp.concatenate([jnp.where(relative == float(b), 1.0, 0.0) for b in range(4)], axis=0)

    for copy in h_copies:
        copy.wait_recv()
    keep_left = jnp.where(jnp.floor(v_left[0:1, 0:1] * 0.25) * 4.0 == label4, 1.0, 0.0)
    keep_right = jnp.where(jnp.floor(v_right[0:1, 0:1] * 0.25) * 4.0 == label4, 1.0, 0.0)
    gf[0:PAD, :] = gvm[0:PAD, :].astype(F32) * keep_left
    gf[PAD:PAD + ROWS, :] = own_g.astype(F32)
    gf[PAD + ROWS:, :] = gvm[PAD + ROWS:, :].astype(F32) * keep_right
    for k in range(KTAP):
        load_w2[k].wait()
        start = PAD - (k - KTAP // 2) * DILATION_SECOND
        term = lax.dot_general(
            gf[start:start + ROWS, :].astype(BF16), w2[k], (((1,), (1,)), ((), ())), preferred_element_type=F32
        )
        acc[...] = term if k == 0 else acc[...] + term
    t_copy.wait_recv()
    tsc[...] = jnp.zeros_like(tsc)
    for k in range(KTAP):
        i = k if k < SHARE else k - SHARE + 1
        seen = jnp.where(core == (0 if k < SHARE else 1), tmine[i], tother[i])
        for b in range(4):
            row = seen[b:b + 1, :]
            if k == KTAP // 2:
                row = row + tab[b:b + 1, :]
            at_row = b * 16 + KTAP - 1 - k
            tsc[at_row:at_row + 1, :] = row
    whole = tsc[...]
    high = whole.astype(BF16).astype(F32)
    middle = (whole - high).astype(BF16).astype(F32)
    low = whole - high - middle
    thirds = jnp.concatenate([high, middle, low], axis=0)
    t3[...] = thirds.astype(BF16)
    t3t[...] = thirds.T.astype(BF16)

    own_hot = onehot(vbuf[0])
    hot_rows = own_hot.T
    hot_rows = jnp.concatenate([hot_rows, hot_rows, hot_rows], axis=1).astype(BF16)
    x1 = jnp.dot(hot_rows, t3[...], preferred_element_type=F32).astype(BF16)
    x1b[...] = x1[PAD:PAD + ROWS, :]
    a2f[...] = jnp.maximum(x1.astype(F32), 0.0)

    dx1 = (gf[PAD:PAD + ROWS, :] + jnp.where(x1b[...].astype(F32) > 0.0, acc[...], 0.0)).astype(BF16)
    sums = jnp.dot(own_hot[:, PAD:PAD + ROWS].astype(BF16), dx1, preferred_element_type=F32)
    first = (lax.broadcasted_iota(jnp.int32, sums.shape, 1) & FOLD) == 0
    sums = jnp.concatenate([jnp.where(first, sums, 0.0), jnp.where(first, 0.0, sums)], axis=0).T
    folded = [sums[i:i + FOLD, :] + sums[i + FOLD:i + SLICE, :] for i in range(0, CH, SLICE)]
    st[...] = jnp.concatenate(folded, axis=0)

    def folds_of(px, py):
        return pl.ds(pl.multiple_of((px * NY + py) * FOLD, FOLD), FOLD)

    s_copies = [
        remote(st.at[folds_of(*group[d])], sbuf.at[d], ssend.at[d], srecv.at[d], at(*group[d], z, core))
        for d in range(1, GROUP)
    ]
    for copy in s_copies:
        copy.start()

    gs[...] = jnp.zeros_like(gs)
    turned_part[...] = jnp.zeros_like(turned_part)
    middle_lanes, left_lanes = 2 * ROWS, 2 * (ROWS + PAD)

    def place(ref, rows, j, block, left_too=True, right_too=True):
        ref[rows, ROWS * j:ROWS * (j + 1)] = block[:, PAD:PAD + ROWS]
        if left_too:
            ref[rows, middle_lanes + PAD * j:middle_lanes + PAD * (j + 1)] = block[:, :PAD]
        if right_too:
            ref[rows, left_lanes + PAD * j:left_lanes + PAD * (j + 1)] = block[:, PAD + ROWS:]

    def pair(i, carry):
        for j in range(2):
            slot = 2 * i + j
            hot = onehot(vbuf[slot]).astype(BF16)
            place(ohs, slice(None), j, jnp.concatenate([hot, hot, hot], axis=0))
            edge = jnp.zeros((SLICE, PAD), F32)
            wide = jnp.concatenate([edge, gbuf[slot].astype(F32), edge], axis=1)
            for k in range(KTAP):
                offset = k - KTAP // 2
                moved = wide if offset == 0 else pltpu.roll(wide, (offset * DILATION_SECOND) % EXT, 1)
                place(gs, slice(SLICE * k, SLICE * (k + 1)), j, moved.astype(BF16), offset < 0, offset > 0)
        hidden = jnp.dot(t3t[...], ohs[...], preferred_element_type=F32)
        a2s[...] = jnp.maximum(hidden, 0.0).astype(BF16)
        before, after = SLICE * (KTAP // 2), SLICE * (KTAP // 2 + 1)
        for rows, lanes in (
            (slice(0, KTAP * SLICE), slice(0, middle_lanes)),
            (slice(0, before), slice(middle_lanes, left_lanes)),
            (slice(after, KTAP * SLICE), slice(left_lanes, 2 * EXT)),
        ):
            turned_part[rows, :] += lax.dot_general(
                gs[rows, lanes], a2s[:, lanes], (((1,), (1,)), ((), ())), preferred_element_type=F32
            )
        return carry

    def pairs(first, last):
        for d in range(max(1, 2 * first), 2 * last):
            g_copies[d - 1].wait_recv()
            b_copies[d - 1].wait_recv()
        lax.fori_loop(first, last, pair, 0)

    pairs(0, 2)
    pairs(2, 4)
    pairs(4, 6)
    for copy in s_copies:
        copy.wait_recv()
    group_sum = st[folds_of(x, y), :]
    for d in range(1, GROUP):
        group_sum = group_sum + sbuf[d]
    ssum[0] = group_sum
    sc_copy = remote(ssum.at[0], screcv, cs.at[1], cr.at[1], at(x, y, z, 1 - core))
    sc_copy.start()
    pairs(6, 7)
    sc_copy.wait_recv()
    ssum[1] = ssum[0] + screcv[...]
    sz_copies = []
    for d in range(1, NZ):
        pz = (z + d) % NZ
        sz_copies.append(remote(ssum.at[1], szrecv.at[d], zsend.at[NZ + d], zrsem.at[NZ + d], at(x, y, pz, core)))
    for copy in sz_copies:
        copy.start()
    pairs(7, 8)
    turned = turned_part[...].T
    order = [(yy * NZ + zz) * NC + cc for cc in range(NC) for zz in range(NZ) for yy in range(NY)]
    part[...] = jnp.concatenate([turned[8 * s:8 * s + 8, :] for s in order], axis=0)

    def half_of(c):
        return pl.ds(pl.multiple_of(c * HALF, HALF), HALF)

    c_copy = remote(part.at[half_of(1 - core)], crecv, cs.at[0], cr.at[0], at(x, y, z, 1 - core))
    c_copy.start()
    c_copy.wait_recv()
    own_half = part[half_of(core), :] + crecv[...]
    part[half_of(core), :] = own_half
    zout[...] = own_half.astype(BF16)

    z_copies = []
    for d in range(1, NZ):
        pz = (z + d) % NZ
        rows = pl.ds(pl.multiple_of(pz * ZROWS, ZROWS), ZROWS)
        z_copies.append(remote(zout.at[rows], zrecv.at[d], zsend.at[d], zrsem.at[d], at(x, y, pz, core)))
    for copy in z_copies:
        copy.start()

    for k in range(KTAP):
        start = PAD + (k - KTAP // 2) * DILATION_SECOND
        term = jnp.dot(a2f[start:start + ROWS, :].astype(BF16), w2[k], preferred_element_type=F32)
        acc[...] = term if k == 0 else acc[...] + term
    fvm[...] = (x1b[...].astype(F32) + acc[...]).astype(BF16)
    store = pltpu.make_async_copy(fvm, feat.at[0], lsem.at[1])
    store.start()

    for copy in sz_copies:
        copy.wait_recv()
    s_total = ssum[1]
    for d in range(1, NZ):
        s_total = s_total + szrecv[d]
    ssum[2] = s_total
    sy_copies = []
    for d in range(1, NY):
        py = (y + d) % NY
        sy_copies.append(remote(ssum.at[2], syrecv.at[y], ys.at[NY + d], yr.at[NY + d], at(x, py, z, core)))
    for copy in sy_copies:
        copy.start()
    syrecv[y] = s_total
    for copy in z_copies:
        copy.wait_recv()
    total = part[pl.ds(pl.multiple_of(core * HALF + z * ZROWS, ZROWS), ZROWS), :]
    for d in range(1, NZ):
        total = total + zrecv[d].astype(F32)
    zs[...] = total


    y_copies = []
    for d in range(1, NY):
        py = (y + d) % NY
        rows = pl.ds(pl.multiple_of(py * 8, 8), 8)
        y_copies.append(remote(zs.at[rows], yrecv.at[y], ys.at[d], yr.at[d], at(x, py, z, core)))
    for copy in y_copies:
        copy.start()
    yrecv[y] = zs[pl.ds(pl.multiple_of(y * 8, 8), 8), :]
    for copy in y_copies + sy_copies:
        copy.wait_recv()

    lane = lax.broadcasted_iota(jnp.int32, (8, PAD), 1)
    unfolded = [side for i in range(NY) for side in (syrecv[i], pltpu.roll(syrecv[i], PAD // 2, 1))]
    by_base = jnp.concatenate(unfolded, axis=0).T
    rows_act = a1t[pl.ds(pl.multiple_of(seq * 8, 8), 8), :]
    for k in range(KTAP):
        block = jnp.zeros((8, PAD), F32)
        for i in range(NY):
            piece = yrecv[i][:, PAD * (k // NY):PAD * (k // NY) + PAD]
            shift = (SLICE * (i - k % NY)) % PAD
            piece = piece if shift == 0 else pltpu.roll(piece, shift, 1)
            block = jnp.where((lane >= SLICE * i) & (lane < SLICE * (i + 1)), piece, block)
        out2[k] = block
        block = jnp.zeros((8, PAD), F32)
        for b in range(4):
            row = b * 16 + KTAP - 1 - k
            block = block + rows_act[:, b:b + 1] * by_base[row:row + 1, :]
        out1[k] = block

    store.wait()
    sent = v_copies + h_copies + g_copies + b_copies + s_copies + [t_copy, c_copy, sc_copy]
    for copy in sent + z_copies + sz_copies + y_copies + sy_copies:
        copy.wait_send()


def hand_over(feat, grad1, grad2, feat_out, out1, out2):
    feat_out[...] = feat[...]
    out1[...] = grad1[...]
    out2[...] = grad2[...]


def body(bases, gene, table, w1, w2, cotangent):
    vm = lambda *shape, dtype=F32: pltpu.VMEM(shape, dtype)
    dma = lambda n: pltpu.SemaphoreType.DMA((n,))
    vmem = pl.BlockSpec(memory_space=pltpu.VMEM)
    hbm = pl.BlockSpec(memory_space=pl.ANY)
    outs = (
        jax.ShapeDtypeStruct((1, ROWS, CH), BF16),
        jax.ShapeDtypeStruct((KTAP, 8, PAD), F32),
        jax.ShapeDtypeStruct((KTAP, 8, PAD), F32),
    )
    results = pl.pallas_call(
        kernel,
        out_shape=outs,
        in_specs=[hbm] * 6,
        out_specs=(hbm, vmem, vmem),
        scratch_shapes=[
            vm(1, ROWS, dtype=jnp.int32),
            vm(1, 1, dtype=jnp.int32),
            vm(4, CH),
            vm(SHARE, CH, CH, dtype=BF16),
            vm(KTAP, CH, CH, dtype=BF16),
            vm(SHARE, 8, CH),
            vm(SHARE, 8, CH),
            vm(EXT, CH, dtype=BF16),
            vm(EXT, CH),
            vm(CH, ROWS, dtype=BF16),
            vm(GROUP, SLICE, ROWS, dtype=BF16),
            vm(3, 8, ROWS),
            vm(GROUP, 8, PAD),
            vm(64, CH),
            vm(192, CH, dtype=BF16),
            vm(CH, 192, dtype=BF16),
            vm(CH, 16),
            vm(192, 2 * EXT, dtype=BF16),
            vm(ROWS, CH, dtype=BF16),
            vm(EXT, CH),
            vm(ROWS, CH),
            vm(ROWS, CH, dtype=BF16),
            vm(CH // 2, PAD),
            vm(GROUP, FOLD, PAD),
            vm(CH, 2 * EXT, dtype=BF16),
            vm(WIDE, 2 * EXT, dtype=BF16),
            vm(WIDE, CH),
            vm(CH, WIDE),
            vm(HALF, WIDE),
            vm(FOLD, PAD),
            vm(HALF, WIDE, dtype=BF16),
            vm(NZ, ZROWS, WIDE, dtype=BF16),
            vm(NZ, FOLD, PAD),
            vm(ZROWS, WIDE),
            vm(3, FOLD, PAD),
            vm(NY, 8, WIDE),
            vm(NY, FOLD, PAD),
            dma(SHARE), dma(KTAP), dma(5), dma(1), dma(1),
            dma(2), dma(2), dma(2), dma(2),
            dma(GROUP), dma(GROUP), dma(GROUP), dma(GROUP), dma(GROUP), dma(GROUP),
            dma(2), dma(2), dma(2 * NZ), dma(2 * NZ), dma(2 * NY), dma(2 * NY),
        ],
        compiler_params=pltpu.CompilerParams(
            collective_id=0, has_side_effects=True, vmem_limit_bytes=60 * 1024 * 1024
        ),
    )(bases, gene, table, cotangent, w1, w2)
    return pl.pallas_call(
        hand_over,
        out_shape=outs,
        in_specs=[vmem, vmem, vmem],
        out_specs=(vmem, vmem, vmem),
    )(*results)


def solution(mesh):
    return jax.shard_map(
        body,
        mesh=mesh,
        in_specs=(P("dp", "seq"), P("dp", "seq"), P(), P(), P(), P("dp", "seq", None)),
        out_specs=(P("dp", "seq", None), P(None, "seq", "dp"), P(None, "seq", "dp")),
        check_vma=False,
    )
```
